32 devices in a mesh: seq: 16 (over z, x, core), section: 2 (over y).
Axes of the slice: x: 2, y: 2, z: 4, core: 2. Of those that a mesh axis runs over, the one named last changes fastest.
Arguments:
- fwd_input: bfloat16 [2, 4096, 768], P('section', 'seq'), may hold values from -6 to 6
- bwd_input: bfloat16 [2, 4096, 768], P('section', 'seq'), may hold values from -6 to 6
- bwd_cotangent: bfloat16 [2, 4096, 768], P('section', 'seq'), may hold values from -6 to 6
- conv_weight: bfloat16 [2, 2, 3, 768, 384], P('section', None, None, 'seq'), may hold values from -0.125 to 0.125
- proj_weight: bfloat16 [2, 2, 384, 768], P('section', None, 'seq'), may hold values from -0.3125 to 0.3125
Outputs:
- next_input: bfloat16 [2, 4096, 768], P('section', 'seq')
- prev_cotangent: bfloat16 [2, 4096, 768], P('section', 'seq')
The draws below stay inside these ranges and needn't reach their ends.
All inputs are finite; a program needn't handle non-finite values.
Results may differ from the reference program's by a relative error of at most 0.012.
Values may be sent and summed in bfloat16 or wider, within the bound.
A program may use at most 64 MiB of HBM per device.

```python
import jax
import jax.numpy as jnp
from jax import lax

C = 768
H = 384
BLOCKS = 2
FIRST_DILATION = 128
POS = 4096
SECTIONS = 2


def block_scale(rng, shape, shards, least, high):
    def one(dim, shards_of):
        heights = jax.random.uniform(jax.random.fold_in(jax.random.fold_in(rng, 6), dim), (shards_of,), jnp.float32, least / len(shards), high / len(shards))
        return jnp.repeat(jnp.exp(heights), shape[dim] // shards_of).reshape((-1,) + (1,) * (len(shape) - dim - 1))

    level = one(*shards[0])
    for cut in shards[1:]:
        level = level * one(*cut)
    return level


def scatter_about(stream_key, shape, scale, most, pieces=(), kind=jnp.bfloat16):
    loudness = block_scale(stream_key, shape, pieces, -0.22, 0.18) if pieces else 1.0
    drawn = jax.random.normal(stream_key, shape, jnp.float32) * scale * loudness
    return jnp.minimum(jnp.maximum(drawn, -most), most).astype(kind)


def setup_inputs(seed: int = 0) -> dict:
    seeds = jax.random.split(jax.random.key(seed), 6)
    fwd_input = scatter_about(seeds[0], (SECTIONS, POS, C), 1.0, 6.0, ((0, 2), (1, 16)))
    bwd_input = scatter_about(seeds[1], (SECTIONS, POS, C), 1.0, 6.0, ((0, 2), (1, 16)))
    bwd_cotangent = scatter_about(seeds[2], (SECTIONS, POS, C), 1.0, 6.0, ((0, 2), (1, 16)))
    conv_weight = scatter_about(seeds[3], (SECTIONS, BLOCKS, 3, C, H), (3 * C) ** -0.5, 0.125, ((0, 2), (3, 16)))
    proj_weight = scatter_about(seeds[4], (SECTIONS, BLOCKS, H, C), H ** -0.5, 0.3125, ((0, 2), (2, 16)))
    return {"fwd_input": fwd_input, "bwd_input": bwd_input, "bwd_cotangent": bwd_cotangent, "conv_weight": conv_weight, "proj_weight": proj_weight}


def spread(values, spacing_gap):
    width = values.shape[1]
    zeros = jnp.zeros((spacing_gap, width), values.dtype)
    earlier = jnp.concatenate([zeros, values[:-spacing_gap]], 0)
    later = jnp.concatenate([values[spacing_gap:], zeros], 0)
    return (earlier, later)

def gelu_back(value, cotangent):
    return jax.vjp(jax.nn.gelu, value)[1](cotangent)[0]

def rounded(product):
    return lax.optimization_barrier(product.astype(jnp.bfloat16)).astype(jnp.float32)

def section_forward(present_state, conv_weight, proj_weight):
    stored = []
    for depth_level in range(BLOCKS):
        spacing_gap = FIRST_DILATION * 4 ** depth_level
        activated = jax.nn.gelu(present_state.astype(jnp.float32)).astype(jnp.bfloat16)
        earlier, later = spread(activated, spacing_gap)
        preact = rounded(jnp.dot(earlier, conv_weight[depth_level, 0], preferred_element_type=jnp.float32))
        preact = preact + jnp.dot(activated, conv_weight[depth_level, 1], preferred_element_type=jnp.float32)
        preact = preact + rounded(jnp.dot(later, conv_weight[depth_level, 2], preferred_element_type=jnp.float32))
        hidden = jax.nn.gelu(preact).astype(jnp.bfloat16)
        stored.append((present_state, preact))
        branch = jnp.dot(hidden, proj_weight[depth_level], preferred_element_type=jnp.float32)
        present_state = (present_state.astype(jnp.float32) + branch).astype(jnp.bfloat16)
    return (present_state, stored)

def section_backward(present_state, cotangent, conv_weight, proj_weight):
    unused, stored = section_forward(present_state, conv_weight, proj_weight)
    for depth_level in reversed(range(BLOCKS)):
        spacing_gap = FIRST_DILATION * 4 ** depth_level
        block_in, preact = stored[depth_level]
        d_hidden = jnp.dot(cotangent, proj_weight[depth_level].T, preferred_element_type=jnp.float32)
        d_preact = gelu_back(preact, d_hidden).astype(jnp.bfloat16)
        earlier, later = spread(d_preact, spacing_gap)
        d_act = jnp.dot(later, conv_weight[depth_level, 0].T, preferred_element_type=jnp.float32)
        d_act = d_act + jnp.dot(d_preact, conv_weight[depth_level, 1].T, preferred_element_type=jnp.float32)
        d_act = d_act + jnp.dot(earlier, conv_weight[depth_level, 2].T, preferred_element_type=jnp.float32)
        total = cotangent.astype(jnp.float32) + gelu_back(block_in.astype(jnp.float32), d_act)
        cotangent = total.astype(jnp.bfloat16)
    return cotangent

def reference(fwd_input, bwd_input, bwd_cotangent, conv_weight, proj_weight):
    forward_results = []
    backward_outs = []
    for section_num in range(SECTIONS):
        result, unused = section_forward(fwd_input[section_num], conv_weight[section_num], proj_weight[section_num])
        forward_results.append(result)
        backward_outs.append(section_backward(bwd_input[section_num], bwd_cotangent[section_num], conv_weight[section_num], proj_weight[section_num]))
    next_input = jnp.roll(jnp.stack(forward_results, 0), 1, axis=0)
    prev_cotangent = jnp.roll(jnp.stack(backward_outs, 0), -1, axis=0)
    return (next_input, prev_cotangent)
```

```python
import functools

import jax
import jax.numpy as jnp
from jax import lax
from jax.experimental import pallas as pl
from jax.experimental.pallas import tpu as pltpu
from jax.sharding import PartitionSpec as P

BLOCKS = 2
FIRST_DILATION = 128
MESH = pl.DeviceIdType.MESH
F32 = jnp.float32
BF16 = jnp.bfloat16
K0 = 0.7978845608028654
K1 = 0.044715
UP, DOWN, ACROSS, SIB = range(4)
CHUNK = 64


def gelu(x):
    return x * (0.5 * (1.0 + jnp.tanh(K0 * (x + K1 * (x * x * x)))))


def gelu_slope(x):
    square = x * x
    t = jnp.tanh(K0 * (x + K1 * (square * x)))
    return 0.5 * (1.0 + t) + x * (0.5 * (1.0 - t * t)) * (K0 * (1.0 + 3.0 * K1 * square))


def dot(a, b):
    return jnp.dot(a, b, preferred_element_type=F32)


def dot_t(a, b):
    return lax.dot_general(a, b, (((1,), (1,)), ((), ())), preferred_element_type=F32)


def by_rows(total, body):
    @pl.loop(0, total // CHUNK)
    def _(j):
        body(pl.ds(pl.multiple_of(j * CHUNK, CHUNK), CHUNK))


def kernel(n, sections, gather, fx, bx, bg, cw, pw, o_next, o_prev, *scratch):
    (wc, pg, pf, act, state, send0, recv0, send1, recv1, pre, slope, dh, e_buf, recv_e1, recv_e0, part, grad,
     out_f, out_b, g_send, g_recv, h_send, h_recv) = scratch
    rows, half = fx.shape[1], FIRST_DILATION
    me, sec = lax.axis_index("seq"), lax.axis_index("section")
    depth = n // 4
    core, chip = lax.rem(me, 2), me // 2
    x, z = lax.rem(chip, 2), chip // 2
    n_z = depth

    def at(zz, xx, cc):
        return (zz * 2 + xx) * 2 + cc

    def to_seq(index):
        return {"seq": index}

    target = {UP: me + 4, DOWN: me - 4, ACROSS: at(z, 1 - x, core), SIB: at(z, x, 1 - core)}

    barrier = pltpu.get_barrier_semaphore()

    def greet(device):
        pl.semaphore_signal(barrier, inc=1, device_id=device, device_id_type=MESH)

    near = [(-1, me >= 1), (1, me < n - 1), (-2, me >= 2), (2, me < n - 2)]
    if gather:
        near += [(-4, z > 0), (4, z < n_z - 1)]
    count = jnp.int32(2)
    for gap, there in near:
        count = count + there.astype(jnp.int32)

        @pl.when(there)
        def _(gap=gap):
            greet(to_seq(me + gap))

    if gather:
        count = count + 2
        greet(to_seq(target[ACROSS]))
        greet(to_seq(target[SIB]))
    next_sec, prev_sec = lax.rem(sec + 1, sections), lax.rem(sec + sections - 1, sections)
    greet({"section": next_sec})
    greet({"section": prev_sec})

    for side, none0, none1 in ((0, me < 1, me < 2), (1, me >= n - 1, me >= n - 2)):
        @pl.when(none0)
        def _(side=side):
            for p in range(2):
                recv0[p, side] = jnp.zeros(recv0.shape[2:], BF16)
            recv_e0[side] = jnp.zeros(recv_e0.shape[1:], BF16)

        @pl.when(none1)
        def _(side=side):
            for p in range(2):
                recv1[p, side] = jnp.zeros(recv1.shape[2:], BF16)
            recv_e1[side] = jnp.zeros(recv_e1.shape[1:], BF16)

    if gather:
        c_rows = cw.shape[3]
        h_rows = pw.shape[2]

        def piece(t, owner):
            if t % 2 == 0:
                return wc.at[t // 2, :, pl.ds(pl.multiple_of(owner * c_rows, 16), c_rows), :]
            return pg.at[t // 2, owner]

        def copy(t, zz, xx, cc, kind):
            owner = at(zz, xx, cc)
            return pltpu.make_async_remote_copy(
                src_ref=piece(t, owner), dst_ref=piece(t, owner),
                send_sem=g_send.at[t, kind, zz * 2 + xx], recv_sem=g_recv.at[t, owner],
                device_id=to_seq(target[kind]), device_id_type=MESH)

        own = pl.ds(pl.multiple_of(me * c_rows, 16), c_rows)
        for b in range(BLOCKS):
            for k in range(3):
                wc[b, k, own, :] = cw[0, b, k]
            p32 = pw[0, b].astype(F32)
            width = p32.shape[1] // 2
            pg[b, me] = jnp.concatenate([p32[:, :width], p32[:, width:]], axis=0).astype(BF16)

        def step(t, k):
            if k == 0:
                @pl.when(z < n_z - 1)
                def _():
                    copy(t, z, x, core, UP).start()

                @pl.when(z > 0)
                def _():
                    copy(t, z, x, core, DOWN).start()
                copy(t, z, x, core, ACROSS).start()
                copy(t, z, x, core, SIB).start()
                return
            if k < n_z:
                @pl.when(z - k >= 0)
                def _():
                    copy(t, z - k, x, core, SIB).wait_recv()

                    @pl.when(z < n_z - 1)
                    def _():
                        copy(t, z - k, x, core, UP).start()
                    copy(t, z - k, x, core, ACROSS).start()
                    copy(t, z - k, x, core, SIB).start()

                @pl.when(z + k < n_z)
                def _():
                    copy(t, z + k, x, core, SIB).wait_recv()

                    @pl.when(z > 0)
                    def _():
                        copy(t, z + k, x, core, DOWN).start()
                    copy(t, z + k, x, core, ACROSS).start()
                    copy(t, z + k, x, core, SIB).start()
            far = k - 1
            if far == 0:
                copy(t, z, 1 - x, core, SIB).wait_recv()
                copy(t, z, 1 - x, core, SIB).start()
            else:
                for zz, there in ((z - far, z - far >= 0), (z + far, z + far < n_z)):
                    @pl.when(there)
                    def _(zz=zz):
                        copy(t, zz, 1 - x, core, SIB).wait_recv()
                        copy(t, zz, 1 - x, core, SIB).start()

        def settle(t):
            for zz in range(n_z):
                for xx in range(2):
                    copy(t, zz, xx, 1 - core, SIB).wait_recv()

        def drain(t):
            for zz in range(n_z):
                @pl.when((zz <= z) & (z < n_z - 1))
                def _(zz=zz):
                    copy(t, zz, x, core, UP).wait_send()

                @pl.when((zz >= z) & (z > 0))
                def _(zz=zz):
                    copy(t, zz, x, core, DOWN).wait_send()
                copy(t, zz, x, core, ACROSS).wait_send()
                for xx in range(2):
                    copy(t, zz, xx, core, SIB).wait_send()

        def join_proj(b):
            for j in range(n // 2):
                tall = []
                for owner in (2 * j, 2 * j + 1):
                    v = pg[b, owner].astype(F32)
                    tall.append(jnp.concatenate([v[:h_rows], v[h_rows:]], axis=1))
                pf[b, 2 * j * h_rows : 2 * (j + 1) * h_rows, :] = jnp.concatenate(tall, axis=0).astype(BF16)

        def conv_w(b, k):
            return wc[b, k]

        def proj_w(b):
            return pf[b]
    else:
        def step(t, k):
            pass

        settle = drain = join_proj = lambda t: None

        def conv_w(b, k):
            return cw[0, b, k]

        def proj_w(b):
            return pw[0, b]

    pl.semaphore_wait(barrier, count)
    step(0, 0)
    step(1, 0)

    def link(slot, src, dst, gap):
        return pltpu.make_async_remote_copy(
            src_ref=src, dst_ref=dst, send_sem=h_send.at[slot], recv_sem=h_recv.at[slot],
            device_id=to_seq(me + gap), device_id_type=MESH)

    def exchange(slot, sources, targets, gap, what):
        for side in range(2):
            ahead = (me < n - gap) if side == 0 else (me >= gap)
            behind = (me >= gap) if side == 0 else (me < n - gap)
            c = functools.partial(link, slot + side, sources[side], targets[side], gap if side == 0 else -gap)
            if what == "start":
                @pl.when(ahead)
                def _(c=c):
                    c().start()
            elif what == "send":
                @pl.when(ahead)
                def _(c=c):
                    c().wait_send()
            else:
                @pl.when(behind)
                def _(c=c):
                    c().wait_recv()

    def halo(b, p, what):
        if b == 0:
            exchange(2 * p, (send0.at[p, 0], send0.at[p, 1]), (recv0.at[p, 0], recv0.at[p, 1]), 1, what)
        else:
            exchange(4 + 2 * p, (send1.at[p, 0], send1.at[p, 1]), (recv1.at[p, 0], recv1.at[p, 1]), 2, what)

    def halo_e(b, what):
        if b == 1:
            exchange(8, (e_buf.at[1], e_buf.at[1]), (recv_e1.at[0], recv_e1.at[1]), 2, what)
        else:
            exchange(10, (e_buf.at[0, pl.ds(rows - half, half)], e_buf.at[0, pl.ds(0, half)]),
                     (recv_e0.at[0], recv_e0.at[1]), 1, what)

    inputs = (fx, bx)

    def activate(p, src):
        def body(r):
            act[p, r, :] = gelu(src[r, :].astype(F32)).astype(BF16)
        by_rows(rows, body)

    def taps(b, p):
        a = act[p]
        q0 = dot(a, conv_w(b, 0)).astype(BF16)
        q2 = dot(a, conv_w(b, 2)).astype(BF16)
        if b == 0:
            send0[p, 0] = q0[rows - half :]
            send0[p, 1] = q2[:half]
            halo(b, p, "start")
            pre[p, :half, :] = q2[half:].astype(F32)
            pre[p, half:, :] = q0[: rows - half].astype(F32)
            pre[p] = pre[p] + dot(a, conv_w(b, 1))
        else:
            send1[p, 0] = q0
            send1[p, 1] = q2
            halo(b, p, "start")
            pre[p] = dot(a, conv_w(b, 1))

    def finish(b, p, r):
        if b == 0:
            raise NotImplementedError
        return pre[p, r, :] + recv1[p, 0, r, :].astype(F32) + recv1[p, 1, r, :].astype(F32)

    def hidden0(p):
        halo(0, p, "recv")
        for side in range(2):
            def body(j, side=side):
                r = pl.ds(side * half + j * CHUNK, CHUNK)
                y = pre[p, r, :] + recv0[p, side, pl.ds(j * CHUNK, CHUNK), :].astype(F32)
                dh[p, r, :] = gelu(y).astype(BF16)
                if p == 1:
                    slope[0, r, :] = gelu_slope(y)
            for j in range(half // CHUNK):
                body(j)

    def advance(p):
        part[...] = dot(dh[p], proj_w(0))
        src = inputs[p]

        def body(r):
            h = (src[0, r, :].astype(F32) + part[r, :]).astype(BF16)
            state[p, r, :] = h
            act[p, r, :] = gelu(h.astype(F32)).astype(BF16)
        by_rows(rows, body)

    activate(1, bx.at[0])
    activate(0, fx.at[0])
    step(0, 1)
    step(1, 1)
    step(2, 0)
    for k in range(2, n_z + 1):
        step(0, k)
        step(1, k)
        if k < n_z:
            step(2, k - 1)
    step(3, 0)
    settle(0)
    taps(0, 1)
    taps(0, 0)
    step(2, n_z - 1)
    step(3, 1)
    settle(1)
    join_proj(0)
    hidden0(1)
    advance(1)
    step(2, n_z)
    step(3, 2)
    hidden0(0)
    advance(0)
    for k in range(3, n_z + 1):
        step(3, k)

    settle(2)
    taps(1, 1)
    taps(1, 0)
    settle(3)
    join_proj(1)
    part_h = part.at[:, pl.ds(0, pre.shape[2])]
    part_h[...] = dot_t(bg[0], proj_w(1))
    halo(1, 1, "recv")

    def body(r):
        e_buf[1, r, :] = (gelu_slope(finish(1, 1, r)) * part[r, : pre.shape[2]]).astype(BF16)
    by_rows(rows, body)
    halo_e(1, "start")

    halo(1, 0, "recv")

    def body(r):
        dh[0, r, :] = gelu(finish(1, 0, r)).astype(BF16)
    by_rows(rows, body)
    part[...] = dot(dh[0], proj_w(1))

    def body(r):
        out_f[r, :] = (state[0, r, :].astype(F32) + part[r, :]).astype(BF16)
    by_rows(rows, body)
    forward = pltpu.make_async_remote_copy(
        src_ref=out_f, dst_ref=o_next.at[0], send_sem=h_send.at[12], recv_sem=h_recv.at[12],
        device_id={"section": next_sec}, device_id_type=MESH)
    forward.start()

    part[...] = dot_t(e_buf[1], conv_w(1, 1))
    halo_e(1, "recv")
    part[...] = part[...] + dot_t(recv_e1[1], conv_w(1, 0)) + dot_t(recv_e1[0], conv_w(1, 2))

    def body(r):
        g = bg[0, r, :].astype(F32) + gelu_slope(state[1, r, :].astype(F32)) * part[r, :]
        grad[r, :] = g.astype(BF16)
    by_rows(rows, body)

    d0 = dot_t(grad[...], proj_w(0))
    e_buf[0] = (slope[0] * d0).astype(BF16)
    halo_e(0, "start")
    e = e_buf[0]
    part[...] = dot_t(e, conv_w(0, 1))
    part[: rows - half, :] = part[: rows - half, :] + dot_t(e_buf[0, half:, :], conv_w(0, 0))
    part[half:, :] = part[half:, :] + dot_t(e_buf[0, : rows - half, :], conv_w(0, 2))
    halo_e(0, "recv")
    part[rows - half :, :] = part[rows - half :, :] + dot_t(recv_e0[1], conv_w(0, 0))
    part[:half, :] = part[:half, :] + dot_t(recv_e0[0], conv_w(0, 2))

    def body(r):
        g = grad[r, :].astype(F32) + gelu_slope(bx[0, r, :].astype(F32)) * part[r, :]
        out_b[r, :] = g.astype(BF16)
    by_rows(rows, body)
    backward = pltpu.make_async_remote_copy(
        src_ref=out_b, dst_ref=o_prev.at[0], send_sem=h_send.at[13], recv_sem=h_recv.at[13],
        device_id={"section": prev_sec}, device_id_type=MESH)
    backward.start()

    for t in range(4):
        drain(t)
    for b in range(2):
        for p in range(2):
            halo(b, p, "send")
        halo_e(b, "send")
    forward.wait()
    backward.wait()


def local(n, sections, fwd_input, bwd_input, bwd_cotangent, conv_weight, proj_weight):
    rows, wide = fwd_input.shape[1:]
    narrow = conv_weight.shape[-1]
    half = FIRST_DILATION
    c_rows, h_rows = conv_weight.shape[3], proj_weight.shape[2]
    gather = c_rows % 16 == 0 and h_rows % 8 == 0
    if not gather:
        conv_weight = lax.all_gather(conv_weight, "seq", axis=3, tiled=True)
        proj_weight = lax.all_gather(proj_weight, "seq", axis=2, tiled=True)
    vm = pltpu.VMEM
    if gather:
        big = [
            vm((BLOCKS, 3, wide, narrow), BF16),
            vm((BLOCKS, n, 2 * h_rows, wide // 2), BF16),
            vm((BLOCKS, narrow, wide), BF16),
        ]
        g_sems = [pltpu.SemaphoreType.DMA((4, 4, n // 2)), pltpu.SemaphoreType.DMA((4, n))]
    else:
        big = [vm((16, 128), BF16)] * 3
        g_sems = [pltpu.SemaphoreType.DMA((1,)), pltpu.SemaphoreType.DMA((1,))]
    scratch = big + [
        vm((2, rows, wide), BF16),
        vm((2, rows, wide), BF16),
        vm((2, 2, half, narrow), BF16),
        vm((2, 2, half, narrow), BF16),
        vm((2, 2, rows, narrow), BF16),
        vm((2, 2, rows, narrow), BF16),
        vm((2, rows, narrow), F32),
        vm((1, rows, narrow), F32),
        vm((2, rows, narrow), BF16),
        vm((2, rows, narrow), BF16),
        vm((2, rows, narrow), BF16),
        vm((2, half, narrow), BF16),
        vm((rows, wide), F32),
        vm((rows, wide), BF16),
        vm((rows, wide), BF16),
        vm((rows, wide), BF16),
        *g_sems,
        pltpu.SemaphoreType.DMA((14,)),
        pltpu.SemaphoreType.DMA((14,)),
    ]
    shape = jax.ShapeDtypeStruct(fwd_input.shape, BF16)
    flops = 24 * 2 * rows * wide * narrow
    return pl.pallas_call(
        functools.partial(kernel, n, sections, gather),
        out_shape=(shape, shape),
        in_specs=[pl.BlockSpec(memory_space=pltpu.VMEM)] * 5,
        out_specs=(pl.BlockSpec(memory_space=pl.ANY),) * 2,
        scratch_shapes=scratch,
        cost_estimate=pl.CostEstimate(flops=flops, bytes_accessed=8 * rows * wide, transcendentals=9 * rows * wide),
        compiler_params=pltpu.CompilerParams(
            collective_id=0, has_side_effects=True, vmem_limit_bytes=48 * 1024 * 1024),
    )(fwd_input, bwd_input, bwd_cotangent, conv_weight, proj_weight)


def solution(mesh):
    in_specs = (
        P("section", "seq", None),
        P("section", "seq", None),
        P("section", "seq", None),
        P("section", None, None, "seq", None),
        P("section", None, "seq", None),
    )
    out_specs = (P("section", "seq", None), P("section", "seq", None))
    body = functools.partial(local, mesh.shape["seq"], mesh.shape["section"])
    return jax.shard_map(body, mesh=mesh, in_specs=in_specs, out_specs=out_specs, check_vma=False)
```

```python
import functools

import jax
import jax.numpy as jnp
from jax import lax
from jax.experimental import pallas as pl
from jax.experimental.pallas import tpu as pltpu
from jax.sharding import PartitionSpec as P

BLOCKS = 2
FIRST_DILATION = 128
MESH = pl.DeviceIdType.MESH
F32 = jnp.float32
BF16 = jnp.bfloat16
K0 = 0.7978845608028654
K1 = 0.044715
UP, DOWN, ACROSS, SIB = range(4)
CHUNK = 64
SLOT = (0, 2, 1)
PIECES = 5
LIGHT = (3, 4)


def gelu(x):
    return x * (0.5 * (1.0 + jnp.tanh(K0 * (x + K1 * (x * x * x)))))


def gelu_slope(x):
    square = x * x
    t = jnp.tanh(K0 * (x + K1 * (square * x)))
    return 0.5 * (1.0 + t) + x * (0.5 * (1.0 - t * t)) * (K0 * (1.0 + 3.0 * K1 * square))


def dot(a, b):
    return jnp.dot(a, b, preferred_element_type=F32)


def dot_t(a, b):
    return lax.dot_general(a, b, (((1,), (1,)), ((), ())), preferred_element_type=F32)


def by_rows(total, body):
    @pl.loop(0, total // CHUNK)
    def _(j):
        body(pl.ds(pl.multiple_of(j * CHUNK, CHUNK), CHUNK))


def kernel(n, sections, gather, fx_hbm, bx_hbm, bg_hbm, cw_hbm, pw_hbm, o_next, o_prev, *scratch):
    (wc, pg, pf, act, state, send0, recv0, send1, recv1, pre, slope, dh, e_buf, recv_e1, recv_e0, part, grad,
     out_f, out_b, fx, bx, bg, pw, g_send, g_recv, h_send, h_recv, l_sem) = scratch
    rows, half = fx.shape[1], FIRST_DILATION
    me, sec = lax.axis_index("seq"), lax.axis_index("section")
    depth = n // 4
    core, chip = lax.rem(me, 2), me // 2
    x, z = lax.rem(chip, 2), chip // 2
    n_z = depth

    def at(zz, xx, cc):
        return (zz * 2 + xx) * 2 + cc

    def to_seq(index):
        return {"seq": index}

    target = {UP: me + 4, DOWN: me - 4, ACROSS: at(z, 1 - x, core), SIB: at(z, x, 1 - core)}

    loads = []

    def load(src, dst):
        c = pltpu.make_async_copy(src, dst, l_sem.at[len(loads)])
        c.start()
        loads.append(c)

    wide_rows = cw_hbm.shape[3]
    own = pl.ds(pl.multiple_of(me * wide_rows, 16), wide_rows) if gather else pl.ds(0, wide_rows)
    load(pw_hbm, pw)
    for b in range(BLOCKS):
        for k in range(3):
            load(cw_hbm.at[0, b, k], wc.at[b, SLOT[k], own, :])
    weight_loads = len(loads)
    for src, dst in ((bx_hbm, bx), (fx_hbm, fx), (bg_hbm, bg)):
        load(src, dst)

    barrier = pltpu.get_barrier_semaphore()

    def greet(device):
        pl.semaphore_signal(barrier, inc=1, device_id=device, device_id_type=MESH)

    near = [(-1, me >= 1), (1, me < n - 1), (-2, me >= 2), (2, me < n - 2)]
    if gather:
        near += [(-4, z > 0), (4, z < n_z - 1)]
    count = jnp.int32(2)
    for gap, there in near:
        count = count + there.astype(jnp.int32)

        @pl.when(there)
        def _(gap=gap):
            greet(to_seq(me + gap))

    if gather:
        count = count + 2
        greet(to_seq(target[ACROSS]))
        greet(to_seq(target[SIB]))
    next_sec, prev_sec = lax.rem(sec + 1, sections), lax.rem(sec + sections - 1, sections)
    greet({"section": next_sec})
    greet({"section": prev_sec})

    for side, none0, none1 in ((0, me < 1, me < 2), (1, me >= n - 1, me >= n - 2)):
        @pl.when(none0)
        def _(side=side):
            for p in range(2):
                recv0[p, side] = jnp.zeros(recv0.shape[2:], BF16)
            recv_e0[side] = jnp.zeros(recv_e0.shape[1:], BF16)

        @pl.when(none1)
        def _(side=side):
            for p in range(2):
                recv1[p, side] = jnp.zeros(recv1.shape[2:], BF16)
            recv_e1[side] = jnp.zeros(recv_e1.shape[1:], BF16)

    if gather:
        c_rows = wide_rows
        h_rows = pw.shape[2]

        def piece(t, owner):
            if t in (1, 4):
                return pg.at[t // 3, owner]
            block, low, taps_held = {0: (0, 0, 3), 2: (1, 0, 2), 3: (1, 2, 1)}[t]
            span = pl.ds(pl.multiple_of(owner * c_rows, 16), c_rows)
            return wc.at[block, pl.ds(low, taps_held), span, :]

        def copy(t, zz, xx, cc, kind):
            owner = at(zz, xx, cc)
            return pltpu.make_async_remote_copy(
                src_ref=piece(t, owner), dst_ref=piece(t, owner),
                send_sem=g_send.at[t, kind, zz * 2 + xx], recv_sem=g_recv.at[t, owner],
                device_id=to_seq(target[kind]), device_id_type=MESH)

        for c in loads[:weight_loads]:
            c.wait()
        for b in range(BLOCKS):
            p32 = pw[0, b].astype(F32)
            width = p32.shape[1] // 2
            pg[b, me] = jnp.concatenate([p32[:, :width], p32[:, width:]], axis=0).astype(BF16)

        def step(t, k):
            if k == 0:
                @pl.when(z < n_z - 1)
                def _():
                    copy(t, z, x, core, UP).start()

                @pl.when(z > 0)
                def _():
                    copy(t, z, x, core, DOWN).start()
                copy(t, z, x, core, ACROSS).start()
                copy(t, z, x, core, SIB).start()
                return
            if t in LIGHT:
                def onward(zz, xx, kind):
                    copy(t, zz, xx, core, SIB).wait_recv()
                    if kind != DOWN:
                        @pl.when(z < n_z - 1)
                        def _():
                            copy(t, zz, xx, core, UP).start()
                    if kind != UP:
                        @pl.when(z > 0)
                        def _():
                            copy(t, zz, xx, core, DOWN).start()
                    copy(t, zz, xx, core, SIB).start()

                if k == 1:
                    onward(z, 1 - x, None)
                for far, xx in ((k, x), (k - 1, 1 - x)):
                    if 0 < far < n_z:
                        @pl.when(z - far >= 0)
                        def _(far=far, xx=xx):
                            onward(z - far, xx, UP)

                        @pl.when(z + far < n_z)
                        def _(far=far, xx=xx):
                            onward(z + far, xx, DOWN)
                return
            if k < n_z:
                @pl.when(z - k >= 0)
                def _():
                    copy(t, z - k, x, core, SIB).wait_recv()

                    @pl.when(z < n_z - 1)
                    def _():
                        copy(t, z - k, x, core, UP).start()
                    copy(t, z - k, x, core, ACROSS).start()
                    copy(t, z - k, x, core, SIB).start()

                @pl.when(z + k < n_z)
                def _():
                    copy(t, z + k, x, core, SIB).wait_recv()

                    @pl.when(z > 0)
                    def _():
                        copy(t, z + k, x, core, DOWN).start()
                    copy(t, z + k, x, core, ACROSS).start()
                    copy(t, z + k, x, core, SIB).start()
            far = k - 1
            if far == 0:
                copy(t, z, 1 - x, core, SIB).wait_recv()
                copy(t, z, 1 - x, core, SIB).start()
            else:
                for zz, there in ((z - far, z - far >= 0), (z + far, z + far < n_z)):
                    @pl.when(there)
                    def _(zz=zz):
                        copy(t, zz, 1 - x, core, SIB).wait_recv()
                        copy(t, zz, 1 - x, core, SIB).start()

        def settle(t):
            for zz in range(n_z):
                for xx in range(2):
                    copy(t, zz, xx, 1 - core, SIB).wait_recv()

        def drain(t):
            light = t in LIGHT
            columns = (x, 1 - x) if light else (x,)
            for zz in range(n_z):
                for xx in columns:
                    @pl.when((zz <= z) & (z < n_z - 1))
                    def _(zz=zz, xx=xx):
                        copy(t, zz, xx, core, UP).wait_send()

                    @pl.when((zz >= z) & (z > 0))
                    def _(zz=zz, xx=xx):
                        copy(t, zz, xx, core, DOWN).wait_send()
                if not light:
                    copy(t, zz, x, core, ACROSS).wait_send()
                for xx in range(2):
                    copy(t, zz, xx, core, SIB).wait_send()
            if light:
                copy(t, z, x, core, ACROSS).wait_send()

        def join_proj(b):
            for j in range(n // 2):
                tall = []
                for owner in (2 * j, 2 * j + 1):
                    v = pg[b, owner].astype(F32)
                    tall.append(jnp.concatenate([v[:h_rows], v[h_rows:]], axis=1))
                pf[b, 2 * j * h_rows : 2 * (j + 1) * h_rows, :] = jnp.concatenate(tall, axis=0).astype(BF16)

        def proj_w(b):
            return pf[b]
    else:
        for c in loads[:weight_loads]:
            c.wait()

        def step(t, k):
            pass

        settle = drain = join_proj = lambda t: None

        def proj_w(b):
            return pw[0, b]

    def conv_w(b, k):
        return wc[b, SLOT[k]]

    pl.semaphore_wait(barrier, count)
    for t in range(3):
        step(t, 0)
    for c in loads[weight_loads:]:
        c.wait()

    def link(slot, src, dst, gap):
        return pltpu.make_async_remote_copy(
            src_ref=src, dst_ref=dst, send_sem=h_send.at[slot], recv_sem=h_recv.at[slot],
            device_id=to_seq(me + gap), device_id_type=MESH)

    def exchange(slot, sources, targets, gap, what):
        for side in range(2):
            ahead = (me < n - gap) if side == 0 else (me >= gap)
            behind = (me >= gap) if side == 0 else (me < n - gap)
            c = functools.partial(link, slot + side, sources[side], targets[side], gap if side == 0 else -gap)
            if what == "start":
                @pl.when(ahead)
                def _(c=c):
                    c().start()
            elif what == "send":
                @pl.when(ahead)
                def _(c=c):
                    c().wait_send()
            else:
                @pl.when(behind)
                def _(c=c):
                    c().wait_recv()

    def halo(b, p, what):
        if b == 0:
            exchange(2 * p, (send0.at[p, 0], send0.at[p, 1]), (recv0.at[p, 0], recv0.at[p, 1]), 1, what)
        else:
            exchange(4 + 2 * p, (send1.at[p, 0], send1.at[p, 1]), (recv1.at[p, 0], recv1.at[p, 1]), 2, what)

    def halo_e(b, what):
        if b == 1:
            exchange(8, (e_buf.at[1], e_buf.at[1]), (recv_e1.at[0], recv_e1.at[1]), 2, what)
        else:
            exchange(10, (e_buf.at[0, pl.ds(rows - half, half)], e_buf.at[0, pl.ds(0, half)]),
                     (recv_e0.at[0], recv_e0.at[1]), 1, what)

    inputs = (fx, bx)

    def activate(p, src):
        def body(r):
            act[p, r, :] = gelu(src[r, :].astype(F32)).astype(BF16)
        by_rows(rows, body)

    def taps(b, p):
        a = act[p]
        q0 = dot(a, conv_w(b, 0)).astype(BF16)
        q2 = dot(a, conv_w(b, 2)).astype(BF16)
        send0[p, 0] = q0[rows - half :]
        send0[p, 1] = q2[:half]
        halo(b, p, "start")
        pre[p, :half, :] = q2[half:].astype(F32)
        pre[p, half:, :] = q0[: rows - half].astype(F32)
        pre[p] = pre[p] + dot(a, conv_w(b, 1))

    def outer(p):
        send1[p, 0] = dot(act[p], conv_w(1, 0)).astype(BF16)
        send1[p, 1] = dot(act[p], conv_w(1, 2)).astype(BF16)
        halo(1, p, "start")

    def finish(b, p, r):
        return pre[p, r, :] + recv1[p, 0, r, :].astype(F32) + recv1[p, 1, r, :].astype(F32)

    def hidden0(p):
        halo(0, p, "recv")
        for side in range(2):
            def body(j, side=side):
                r = pl.ds(side * half + j * CHUNK, CHUNK)
                y = pre[p, r, :] + recv0[p, side, pl.ds(j * CHUNK, CHUNK), :].astype(F32)
                dh[p, r, :] = gelu(y).astype(BF16)
                if p == 1:
                    slope[0, r, :] = gelu_slope(y)
            for j in range(half // CHUNK):
                body(j)

    def advance(p):
        part[...] = dot(dh[p], proj_w(0))
        src = inputs[p]

        def body(r):
            h = (src[0, r, :].astype(F32) + part[r, :]).astype(BF16)
            state[p, r, :] = h
            act[p, r, :] = gelu(h.astype(F32)).astype(BF16)
        by_rows(rows, body)

    activate(1, bx.at[0])
    activate(0, fx.at[0])
    for k in range(1, n_z + 1):
        step(0, k)
        step(1, k)
        if k == 1:
            step(3, 0)
            step(4, 0)
        else:
            for t in range(2, PIECES):
                step(t, k - 1)
    settle(0)
    taps(0, 1)
    step(2, n_z)
    taps(0, 0)
    step(3, n_z)
    step(4, n_z)
    settle(1)
    join_proj(0)
    hidden0(1)
    advance(1)
    hidden0(0)
    advance(0)

    settle(2)
    outer(1)
    outer(0)
    settle(3)
    pre[1] = dot(act[1], conv_w(1, 1))
    pre[0] = dot(act[0], conv_w(1, 1))
    settle(4)
    join_proj(1)
    part_h = part.at[:, pl.ds(0, pre.shape[2])]
    part_h[...] = dot_t(bg[0], proj_w(1))
    halo(1, 1, "recv")

    def body(r):
        e_buf[1, r, :] = (gelu_slope(finish(1, 1, r)) * part[r, : pre.shape[2]]).astype(BF16)
    by_rows(rows, body)
    halo_e(1, "start")

    halo(1, 0, "recv")

    def body(r):
        dh[0, r, :] = gelu(finish(1, 0, r)).astype(BF16)
    by_rows(rows, body)
    part[...] = dot(dh[0], proj_w(1))

    chunks = rows // CHUNK

    def ship(j, held, out, slot, section):
        r = pl.ds(j * CHUNK, CHUNK)
        return pltpu.make_async_remote_copy(
            src_ref=held.at[r, :], dst_ref=out.at[0, r, :], send_sem=h_send.at[slot + j], recv_sem=h_recv.at[slot + j],
            device_id={"section": section}, device_id_type=MESH)

    for j in range(chunks):
        r = pl.ds(j * CHUNK, CHUNK)
        out_f[r, :] = (state[0, r, :].astype(F32) + part[r, :]).astype(BF16)
        ship(j, out_f, o_next, 12, next_sec).start()

    part[...] = dot_t(e_buf[1], conv_w(1, 1))
    halo_e(1, "recv")
    part[...] = part[...] + dot_t(recv_e1[1], conv_w(1, 0)) + dot_t(recv_e1[0], conv_w(1, 2))

    def body(r):
        g = bg[0, r, :].astype(F32) + gelu_slope(state[1, r, :].astype(F32)) * part[r, :]
        grad[r, :] = g.astype(BF16)
    by_rows(rows, body)

    d0 = dot_t(grad[...], proj_w(0))
    e_buf[0] = (slope[0] * d0).astype(BF16)
    halo_e(0, "start")
    e = e_buf[0]
    part[...] = dot_t(e, conv_w(0, 1))
    part[: rows - half, :] = part[: rows - half, :] + dot_t(e_buf[0, half:, :], conv_w(0, 0))
    part[half:, :] = part[half:, :] + dot_t(e_buf[0, : rows - half, :], conv_w(0, 2))
    halo_e(0, "recv")
    part[rows - half :, :] = part[rows - half :, :] + dot_t(recv_e0[1], conv_w(0, 0))
    part[:half, :] = part[:half, :] + dot_t(recv_e0[0], conv_w(0, 2))

    for j in range(chunks):
        r = pl.ds(j * CHUNK, CHUNK)
        g = grad[r, :].astype(F32) + gelu_slope(bx[0, r, :].astype(F32)) * part[r, :]
        out_b[r, :] = g.astype(BF16)
        ship(j, out_b, o_prev, 12 + chunks, prev_sec).start()

    for t in range(PIECES):
        drain(t)
    for b in range(2):
        for p in range(2):
            halo(b, p, "send")
        halo_e(b, "send")
    for j in range(chunks):
        ship(j, out_f, o_next, 12, next_sec).wait()
        ship(j, out_b, o_prev, 12 + chunks, prev_sec).wait()


def local(n, sections, fwd_input, bwd_input, bwd_cotangent, conv_weight, proj_weight):
    rows, wide = fwd_input.shape[1:]
    narrow = conv_weight.shape[-1]
    half = FIRST_DILATION
    c_rows, h_rows = conv_weight.shape[3], proj_weight.shape[2]
    gather = c_rows % 16 == 0 and h_rows % 8 == 0
    if not gather:
        conv_weight = lax.all_gather(conv_weight, "seq", axis=3, tiled=True)
        proj_weight = lax.all_gather(proj_weight, "seq", axis=2, tiled=True)
    vm = pltpu.VMEM
    if gather:
        big = [
            vm((BLOCKS, 3, wide, narrow), BF16),
            vm((BLOCKS, n, 2 * h_rows, wide // 2), BF16),
            vm((BLOCKS, narrow, wide), BF16),
        ]
        g_sems = [pltpu.SemaphoreType.DMA((PIECES, 4, n // 2)), pltpu.SemaphoreType.DMA((PIECES, n))]
    else:
        big = [vm((BLOCKS, 3, wide, narrow), BF16), vm((16, 128), BF16), vm((16, 128), BF16)]
        g_sems = [pltpu.SemaphoreType.DMA((1,)), pltpu.SemaphoreType.DMA((1,))]
    scratch = big + [
        vm((2, rows, wide), BF16),
        vm((2, rows, wide), BF16),
        vm((2, 2, half, narrow), BF16),
        vm((2, 2, half, narrow), BF16),
        vm((2, 2, rows, narrow), BF16),
        vm((2, 2, rows, narrow), BF16),
        vm((2, rows, narrow), F32),
        vm((1, rows, narrow), F32),
        vm((2, rows, narrow), BF16),
        vm((2, rows, narrow), BF16),
        vm((2, rows, narrow), BF16),
        vm((2, half, narrow), BF16),
        vm((rows, wide), F32),
        vm((rows, wide), BF16),
        vm((rows, wide), BF16),
        vm((rows, wide), BF16),
        *[vm((1, rows, wide), BF16)] * 3,
        vm(proj_weight.shape, BF16),
        *g_sems,
        pltpu.SemaphoreType.DMA((12 + 2 * (rows // CHUNK),)),
        pltpu.SemaphoreType.DMA((12 + 2 * (rows // CHUNK),)),
        pltpu.SemaphoreType.DMA((10,)),
    ]
    shape = jax.ShapeDtypeStruct(fwd_input.shape, BF16)
    flops = 24 * 2 * rows * wide * narrow
    return pl.pallas_call(
        functools.partial(kernel, n, sections, gather),
        out_shape=(shape, shape),
        in_specs=[pl.BlockSpec(memory_space=pltpu.HBM)] * 5,
        out_specs=(pl.BlockSpec(memory_space=pl.ANY),) * 2,
        scratch_shapes=scratch,
        cost_estimate=pl.CostEstimate(flops=flops, bytes_accessed=8 * rows * wide, transcendentals=9 * rows * wide),
        compiler_params=pltpu.CompilerParams(
            collective_id=0, has_side_effects=True, vmem_limit_bytes=62 * 1024 * 1024),
    )(fwd_input, bwd_input, bwd_cotangent, conv_weight, proj_weight)


def solution(mesh):
    in_specs = (
        P("section", "seq", None),
        P("section", "seq", None),
        P("section", "seq", None),
        P("section", None, None, "seq", None),
        P("section", None, "seq", None),
    )
    out_specs = (P("section", "seq", None), P("section", "seq", None))
    body = functools.partial(local, mesh.shape["seq"], mesh.shape["section"])
    return jax.shard_map(body, mesh=mesh, in_specs=in_specs, out_specs=out_specs, check_vma=False)
```
